32 devices in a mesh: groups: 2 (over x), dp: 8 (over z, y), expert: 2 (over core).
Axes of the slice: x: 2, y: 2, z: 4, core: 2. Of those that a mesh axis runs over, the one named last changes fastest.
Arguments:
- tokens: bfloat16 [1024, 3072], P(('groups', 'expert')), parts along dimension 0, may hold values from -6 to 6
- router_weight: bfloat16 [3072, 4], replicated, may hold values from -0.109375 to 0.109375
- w_gate: bfloat16 [4, 3072, 16384], P('expert', None, 'dp'), may hold values from -0.109375 to 0.109375
- w_up: bfloat16 [4, 3072, 16384], P('expert', None, 'dp'), may hold values from -0.109375 to 0.109375
- w_down: bfloat16 [4, 16384, 3072], P('expert', 'dp'), may hold values from -0.046875 to 0.046875
- expert_ids: int32 [1024, 2], P(('groups', 'expert')), parts along dimension 0, may hold values from 0 to 3, all different within a row; in each aligned block of 256 rows (0 to 255, 256 to 511, ...) at most 192 rows name the same one
- positions: int32 [32], P('groups'), parts along dimension 0, may hold values from 0 to 511, as said below
- embed: float32 [32, 4096], P('groups'), parts along dimension 0, may hold values from -6 to 6
- w_first: float32 [3072, 4096], P(('dp', 'expert')), may hold values from -0.09375 to 0.09375
- w_second: float32 [3072, 3072], P(('dp', 'expert')), may hold values from -0.109375 to 0.109375
- cotangent: bfloat16 [32, 3072], P('groups'), parts along dimension 0, may hold values from -6 to 6
Outputs:
- mixed: bfloat16 [2, 512, 3072], P('expert', ('groups', 'dp')), parts along dimension 1
- grad_first: float32 [6144, 4096], P(('groups', 'dp', 'expert')), parts along dimension 0
- grad_second: float32 [6144, 3072], P(('groups', 'dp', 'expert')), parts along dimension 0
The draws below stay inside these ranges and needn't reach their ends.
There are 2 independent parts, one for each index of `groups`. The reference program is written for one: setup_inputs(seed, part) draws one part's arguments, and reference() takes and returns one part's arrays. A program takes and returns all parts, laid end to end along the dimension named above; an argument that names none is the same for every part. Nothing has to cross between parts.
Inputs may be any that keep to these rules, and one draw needn't show every extreme that they name: `expert_ids`: within the 256 rows of one device no expert is named by more than 192 rows, and in some device's rows one expert is named by exactly 192; the two experts of a row differ. `positions`: 16 distinct token slots.
All inputs are finite; a program needn't handle non-finite values.
Results may differ from the reference program's by a relative error of at most 0.008.
Values may be sent and summed in bfloat16 or wider, within the bound.
A program may use at most 256 MiB of HBM per device.

```python
import math
import jax
import jax.numpy as jnp
import numpy as np
from jax import lax

D = 3072
FF = 16384
EXPERTS = 4
TOP = 2
EMB = 4096
PH = 3072
TOK_DEV = 256
DOCS = 16
CAP = 192
TOKENS = 512
N_EXPERT = 2


def draw_positions(key, part):
    key = jax.random.fold_in(key, 11)
    shuffled = jax.random.permutation(key, TOKENS)
    return shuffled[:DOCS].astype(jnp.int32)


def level_of(key, shape, pieces, least, high):
    loudness = 1.0
    for dim, parts in pieces:
        heights = jax.random.uniform(jax.random.fold_in(jax.random.fold_in(key, 6), dim), (parts,), jnp.float32, least / len(pieces), high / len(pieces))
        loudness = loudness * jnp.repeat(jnp.exp(heights), shape[dim] // parts).reshape((-1,) + (1,) * (len(shape) - 1 - dim))
    return loudness


def shared_out(own_key, own, number, rows, count, top, limit, skew):
    ranking = jax.random.permutation(own_key, count)
    packed, usual = portions_of(count, rows * top, limit, skew, True), portions_of(count, rows * top, limit, skew, False)
    places = jnp.arange(count)

    def named(tallies, rotation):
        used = int((tallies > 0).sum())
        fixed = max(1, used // 4)
        passed = fixed + (places - fixed + rotation * (used - fixed)) % max(1, count - fixed)
        return jnp.zeros((count,), jnp.int32).at[ranking[jnp.where(places < fixed, places, passed)]].set(jnp.asarray(tallies, jnp.int32))

    tallies = jnp.where(number % 4 == 0, named(packed, number // 4), named(usual, number - number // 4 - 1))
    mixed = jax.random.permutation(jax.random.fold_in(own, 3), count)
    donor, taker = mixed[0:count // 2 * 2:2], mixed[1:count // 2 * 2:2]
    slack = jnp.minimum(tallies[donor] - 1, limit - tallies[taker]) // 2
    slack = jnp.where((donor == ranking[0]) | (taker == ranking[0]) | (tallies[taker] == 0), 0, jnp.maximum(slack, 0))
    passed = jax.random.randint(jax.random.fold_in(own, 4), (count // 2,), 0, 1 << 20) % (slack + 1)
    tallies = tallies.at[donor].add(-passed).at[taker].add(passed)
    items = jnp.searchsorted(jnp.cumsum(tallies), jnp.arange(rows * top), side="right").astype(jnp.int32)
    listing = items.reshape(top, rows).T
    listing = listing[jax.random.permutation(jax.random.fold_in(own, 1), rows)]
    rotation = jax.random.randint(jax.random.fold_in(own, 2), (rows, 1), 0, top)
    return jnp.take_along_axis(listing, (jnp.arange(top)[None, :] + rotation) % top, axis=1)


def portions_of(count, total, limit, lean, full):
    weights = [(1 << 20) // math.isqrt(standing ** lean) + 1 for standing in range(1, count + 1)]
    largest = limit if full else min(limit, max(-(-total // count), total * weights[0] // sum(weights)))
    least = 1 if total - largest >= count - 1 else 0
    holding, spare = [largest] + [least] * (count - 1), total - largest - least * (count - 1)
    while spare > 0:
        movable = [i for i in range(1, count) if holding[i] < largest] or [i for i in range(1, count) if holding[i] < limit]
        pool, left = sum([weights[i] for i in movable]), spare
        for i in movable:
            extra = min(limit - holding[i], max(1, left * weights[i] // pool), spare)
            holding[i] = holding[i] + extra
            spare = spare - extra
    return np.array(holding)


def bell_draw(own_key, dims, width, limit, pieces=(), kind=jnp.bfloat16):
    values = jax.random.normal(own_key, dims, jnp.float32) * width
    if len(pieces) > 0:
        values = level_of(own_key, dims, pieces, -0.22, 0.18) * values
    return jnp.clip(values, min=-limit, max=limit).astype(kind)


def setup_inputs(seed: int = 0, part: int = 0) -> dict:
    splits = jax.random.split(jax.random.key(seed), 12)
    part_keys = jax.random.split(jax.random.fold_in(splits[11], part), 12)
    tokens = bell_draw(part_keys[0], (TOKENS, D), 1.0, 6.0, ((0, 2),))
    router_weight = bell_draw(splits[1], (D, EXPERTS), D ** -0.5, 0.109375)
    w_gate = bell_draw(splits[2], (EXPERTS, D, FF), D ** -0.5, 0.109375, ((0, 2), (2, 8)))
    w_up = bell_draw(splits[3], (EXPERTS, D, FF), D ** -0.5, 0.109375, ((0, 2), (2, 8)))
    w_down = bell_draw(splits[4], (EXPERTS, FF, D), FF ** -0.5, 0.046875, ((0, 2), (1, 8)))
    expert_ids_keys = jax.random.split(jax.random.fold_in(part_keys[5], 1), TOKENS // TOK_DEV)
    expert_ids_turns = jax.random.permutation(jax.random.fold_in(part_keys[5], 3), TOKENS // TOK_DEV)
    expert_ids = jax.vmap(lambda own, number: shared_out(jax.random.fold_in(part_keys[5], 2), own, number, TOK_DEV, EXPERTS, TOP, CAP, 2))(expert_ids_keys, expert_ids_turns).reshape((TOKENS, TOP))
    positions = draw_positions(jax.random.fold_in(jax.random.fold_in(splits[11], part), 71), part)
    embed = bell_draw(part_keys[7], (DOCS, EMB), 1.0, 6.0, (), jnp.float32)
    w_first = bell_draw(splits[8], (PH, EMB), EMB ** -0.5, 0.09375, ((0, 16),), jnp.float32)
    w_second = bell_draw(splits[9], (PH, D), PH ** -0.5, 0.109375, ((0, 16),), jnp.float32)
    cotangent = bell_draw(part_keys[10], (DOCS, D), 1.0, 6.0)
    return dict(tokens=tokens, router_weight=router_weight, w_gate=w_gate, w_up=w_up, w_down=w_down, expert_ids=expert_ids, positions=positions, embed=embed, w_first=w_first, w_second=w_second, cotangent=cotangent)


PRECISE = lax.Precision.HIGHEST


def gelu_slope(values):
    normal_cdf = 0.5 * (1.0 + jax.scipy.special.erf(values * 0.7071067811865476))
    density = jnp.exp(-0.5 * values * values) * 0.3989422804014327
    return normal_cdf + values * density


def silu_slope(values):
    sigma = jax.nn.sigmoid(values)
    return sigma * (1.0 + values * (1.0 - sigma))


def gate_table(logits, mask):
    chosen_sum = jnp.sum(mask * logits, axis=1, keepdims=True)
    return mask * jax.nn.sigmoid(2.0 * logits - chosen_sum)


def reference(tokens, router_weight, w_gate, w_up, w_down, expert_ids, positions, embed, w_first, w_second, cotangent):
    pre_act = jnp.dot(embed, w_first.T, precision=PRECISE)
    activated = jax.nn.gelu(pre_act, approximate=False)
    projected = jnp.dot(activated, w_second, precision=PRECISE)
    doc_rows = projected.astype(jnp.bfloat16)
    inputs = tokens.at[positions].set(doc_rows)
    expert_range = jnp.arange(EXPERTS, dtype=jnp.int32)
    route_mask = jnp.sum((expert_ids[:, :, None] == expert_range[None, None, :]).astype(jnp.float32), axis=1)
    logits = jnp.dot(inputs, router_weight, preferred_element_type=jnp.float32)
    gates = gate_table(logits, route_mask)
    doc_gates = gates[positions]
    cot_float = cotangent.astype(jnp.float32)
    mixed = jnp.zeros((TOKENS, D), jnp.float32)
    expert_grad = jnp.zeros((DOCS, D), jnp.float32)
    score_list = []
    for expert in range(EXPERTS):
        gate_pre = jnp.dot(inputs, w_gate[expert], preferred_element_type=jnp.float32)
        up_pre = jnp.dot(inputs, w_up[expert], preferred_element_type=jnp.float32)
        expert_hidden = (jax.nn.silu(gate_pre) * up_pre).astype(jnp.bfloat16)
        expert_out = jnp.dot(expert_hidden, w_down[expert], preferred_element_type=jnp.float32)
        mixed = mixed + gates[:, expert:expert + 1] * expert_out
        score_list.append(jnp.sum(cot_float * expert_out[positions], axis=1))
        doc_gate_pre = gate_pre[positions]
        doc_up_pre = up_pre[positions]
        back_proj = jnp.dot(cotangent, w_down[expert].T, preferred_element_type=jnp.float32)
        scaled = doc_gates[:, expert:expert + 1] * back_proj
        up_grad = (scaled * jax.nn.silu(doc_gate_pre)).astype(jnp.bfloat16)
        gate_grad = (scaled * doc_up_pre * silu_slope(doc_gate_pre)).astype(jnp.bfloat16)
        expert_grad = expert_grad + jnp.dot(gate_grad, w_gate[expert].T, preferred_element_type=jnp.float32)
        expert_grad = expert_grad + jnp.dot(up_grad, w_up[expert].T, preferred_element_type=jnp.float32)
    scores = jnp.stack(score_list, axis=1)
    centre = jnp.sum(doc_gates * scores, axis=1, keepdims=True)
    router_grad = doc_gates * (scores - centre)
    grad_proj = expert_grad + jnp.dot(router_grad, router_weight.astype(jnp.float32).T, precision=PRECISE)
    grad_second = jnp.dot(activated.T, grad_proj, precision=PRECISE)
    grad_hidden = jnp.dot(grad_proj, w_second.T, precision=PRECISE) * gelu_slope(pre_act)
    grad_first = jnp.dot(grad_hidden.T, embed, precision=PRECISE)
    mixed_out = mixed.astype(jnp.bfloat16).reshape(N_EXPERT, TOK_DEV, D)
    return mixed_out, grad_first, grad_second
```

```python
import functools

import jax
import jax.numpy as jnp
from jax import lax
from jax.experimental import pallas as pl
from jax.experimental.pallas import tpu as pltpu
from jax.sharding import PartitionSpec as P

EXPERTS = 4
PRECISE = lax.Precision.HIGHEST
LANES = 128
FF_TILE = 512
VMEM_BYTES = 60 * 1024 * 1024


def gelu_slope(values):
    normal_cdf = 0.5 * (1.0 + jax.scipy.special.erf(values * 0.7071067811865476))
    density = jnp.exp(-0.5 * values * values) * 0.3989422804014327
    return normal_cdf + values * density


def gate_table(logits, mask):
    chosen_sum = jnp.sum(mask * logits, axis=1, keepdims=True)
    return mask * jax.nn.sigmoid(2.0 * logits - chosen_sum)


def contract_last(left, right):
    return lax.dot_general(
        left, right, (((1,), (1,)), ((), ())), preferred_element_type=jnp.float32
    )


def sum_kernel(dp_count, halves, x_ref, out_ref, land, total, sems):
    count = dp_count * halves
    me = lax.axis_index("dp") * halves + lax.axis_index("expert")

    def place(step):
        other = lax.rem(me + step, count)
        return other, {"dp": other // halves, "expert": lax.rem(other, halves)}

    barrier = pltpu.get_barrier_semaphore()
    for step in range(1, count):
        pl.semaphore_signal(
            barrier, inc=1, device_id=place(step)[1], device_id_type=pl.DeviceIdType.MESH
        )
    pl.semaphore_wait(barrier, count - 1)

    def scatter(step):
        other, device = place(step)
        return pltpu.make_async_remote_copy(
            src_ref=x_ref.at[other],
            dst_ref=land.at[step],
            send_sem=sems.at[0, step],
            recv_sem=sems.at[1, step],
            device_id=device,
            device_id_type=pl.DeviceIdType.MESH,
        )

    def spread(step):
        return pltpu.make_async_remote_copy(
            src_ref=total.at[me],
            dst_ref=total.at[me],
            send_sem=sems.at[2, step],
            recv_sem=sems.at[3, step],
            device_id=place(step)[1],
            device_id_type=pl.DeviceIdType.MESH,
        )

    for step in range(1, count):
        scatter(step).start()
    acc = x_ref[me]
    for step in range(1, count):
        scatter(step).wait_recv()
        acc = acc + land[step]
    total[me] = acc
    for step in range(1, count):
        spread(step).start()
    for step in range(1, count):
        scatter(step).wait_send()
    for step in range(1, count):
        spread(step).wait()
    out_ref[...] = total[...]


def sum_all(x, collective_id):
    dp_count = lax.axis_size("dp")
    halves = lax.axis_size("expert")
    count = dp_count * halves
    rows = x.shape[1]
    return pl.pallas_call(
        functools.partial(sum_kernel, dp_count, halves),
        out_shape=jax.ShapeDtypeStruct(x.shape, x.dtype),
        in_specs=[pl.BlockSpec(memory_space=pltpu.VMEM)],
        out_specs=pl.BlockSpec(memory_space=pltpu.VMEM),
        scratch_shapes=[
            pltpu.VMEM((count, rows, LANES), x.dtype),
            pltpu.VMEM((count, rows, LANES), x.dtype),
            pltpu.SemaphoreType.DMA((4, count)),
        ],
        compiler_params=pltpu.CompilerParams(
            collective_id=collective_id, has_side_effects=True
        ),
    )(x)


def expert_kernel(
    tok_count,
    rows_ref,
    gates_ref,
    doc_gates_ref,
    cot_ref,
    w_gate_ref,
    w_up_ref,
    w_down_ref,
    mixed_ref,
    grad_ref,
    score_ref,
):
    first = (pl.program_id(0) == 0) & (pl.program_id(1) == 0)

    @pl.when(first)
    def _():
        mixed_ref[...] = jnp.zeros_like(mixed_ref)
        grad_ref[...] = jnp.zeros_like(grad_ref)

    @pl.when(pl.program_id(1) == 0)
    def _():
        score_ref[...] = jnp.zeros_like(score_ref)

    rows = rows_ref[...]
    w_gate = w_gate_ref[0]
    w_up = w_up_ref[0]
    w_down = w_down_ref[0]
    gate_pre = jnp.dot(rows, w_gate, preferred_element_type=jnp.float32)
    up_pre = jnp.dot(rows, w_up, preferred_element_type=jnp.float32)
    sigma = jax.nn.sigmoid(gate_pre)
    silu = gate_pre * sigma
    product = silu * up_pre
    hidden = (product[:tok_count] * gates_ref[0]).astype(jnp.bfloat16)
    mixed_ref[...] += jnp.dot(hidden, w_down, preferred_element_type=jnp.float32)
    doc_gate = gate_pre[tok_count:]
    doc_up = up_pre[tok_count:]
    doc_sigma = sigma[tok_count:]
    doc_silu = silu[tok_count:]
    doc_hidden = product[tok_count:].astype(jnp.bfloat16).astype(jnp.float32)
    back = contract_last(cot_ref[...], w_down)
    score = jnp.sum(doc_hidden * back, axis=1, keepdims=True)
    score_ref[0] += jnp.broadcast_to(score, score_ref.shape[1:])
    scaled = back * doc_gates_ref[0]
    up_grad = (scaled * doc_silu).astype(jnp.bfloat16)
    slope = doc_sigma * (1.0 + doc_gate * (1.0 - doc_sigma))
    gate_grad = (scaled * doc_up * slope).astype(jnp.bfloat16)
    grad_ref[...] += contract_last(gate_grad, w_gate) + contract_last(up_grad, w_up)


def run_experts(rows, gates, doc_gates, cotangent, w_gate, w_up, w_down):
    local_count, width, ff = w_gate.shape
    tok_count = gates.shape[1]
    docs_count = cotangent.shape[0]
    tile = min(FF_TILE, ff)
    fixed = lambda e, f: (0, 0)
    of_expert = lambda e, f: (e, 0, 0)
    return pl.pallas_call(
        functools.partial(expert_kernel, tok_count),
        grid=(local_count, ff // tile),
        out_shape=(
            jax.ShapeDtypeStruct((tok_count, width), jnp.float32),
            jax.ShapeDtypeStruct((docs_count, width), jnp.float32),
            jax.ShapeDtypeStruct((local_count, docs_count, LANES), jnp.float32),
        ),
        in_specs=[
            pl.BlockSpec(rows.shape, fixed),
            pl.BlockSpec((1, tok_count, 1), of_expert),
            pl.BlockSpec((1, docs_count, 1), of_expert),
            pl.BlockSpec(cotangent.shape, fixed),
            pl.BlockSpec((1, width, tile), lambda e, f: (e, 0, f)),
            pl.BlockSpec((1, width, tile), lambda e, f: (e, 0, f)),
            pl.BlockSpec((1, tile, width), lambda e, f: (e, f, 0)),
        ],
        out_specs=(
            pl.BlockSpec((tok_count, width), fixed),
            pl.BlockSpec((docs_count, width), fixed),
            pl.BlockSpec((1, docs_count, LANES), of_expert),
        ),
        compiler_params=pltpu.CompilerParams(vmem_limit_bytes=VMEM_BYTES),
    )(rows, gates, doc_gates, cotangent, w_gate, w_up, w_down)


def body(
    tokens,
    router_weight,
    w_gate,
    w_up,
    w_down,
    expert_ids,
    positions,
    embed,
    w_first,
    w_second,
    cotangent,
):
    tok_rows, width = tokens.shape
    local_count = w_gate.shape[0]
    docs_count = positions.shape[0]
    halves = lax.axis_size("expert")
    dp_count = lax.axis_size("dp")
    count = halves * dp_count
    out_rows = tok_rows // dp_count
    half = lax.axis_index("expert")
    expert_base = half * local_count
    swap = [(0, 1), (1, 0)]

    all_tokens = jnp.concatenate([tokens, lax.ppermute(tokens, "expert", swap)], axis=0)
    all_ids = jnp.concatenate([expert_ids, lax.ppermute(expert_ids, "expert", swap)], axis=0)
    span = jnp.arange(tok_rows, dtype=jnp.int32)
    row_index = jnp.concatenate([half * tok_rows + span, (1 - half) * tok_rows + span])
    expert_range = jnp.arange(EXPERTS, dtype=jnp.int32)
    choose = (all_ids[:, :, None] == expert_range[None, None, :]).astype(jnp.float32)
    route_mask = jnp.sum(choose, axis=1)
    match = (row_index[:, None] == positions[None, :]).astype(jnp.float32)
    doc_mask = jnp.dot(match.T, route_mask, precision=PRECISE)

    pre_act = lax.dot_general(embed, w_first, (((1,), (1,)), ((), ())), precision=PRECISE)
    activated = jax.nn.gelu(pre_act, approximate=False)
    partial = jnp.dot(activated, w_second, precision=PRECISE)
    projected = sum_all(partial.reshape(count, -1, LANES), 1).reshape(docs_count, width)
    doc_rows = projected.astype(jnp.bfloat16)
    placed = jnp.dot(match.astype(jnp.bfloat16), doc_rows, preferred_element_type=jnp.float32)
    present = jnp.sum(match, axis=1, keepdims=True) > 0.5
    inputs = jnp.where(present, placed.astype(jnp.bfloat16), all_tokens)
    rows = jnp.concatenate([inputs, doc_rows], axis=0)
    logits = jnp.dot(rows, router_weight, preferred_element_type=jnp.float32)
    gates = gate_table(logits, jnp.concatenate([route_mask, doc_mask], axis=0))
    own_gates = lax.dynamic_slice_in_dim(gates, expert_base, local_count, 1).T[:, :, None]
    tok_count = halves * tok_rows
    doc_gates = gates[tok_count:]

    mixed_part, expert_grad, score_local = run_experts(
        rows,
        own_gates[:, :tok_count],
        own_gates[:, tok_count:],
        cotangent,
        w_gate,
        w_up,
        w_down,
    )
    given = lax.ppermute(mixed_part[tok_rows:].astype(jnp.bfloat16), "expert", swap)
    pair_sum = mixed_part[:tok_rows] + given.astype(jnp.float32)
    summed = lax.psum_scatter(pair_sum, "dp", scatter_dimension=0, tiled=True)
    mixed = summed.astype(jnp.bfloat16).reshape(1, out_rows, width)

    score_part = lax.dynamic_update_slice_in_dim(
        jnp.zeros((docs_count, EXPERTS), jnp.float32), score_local[:, :, 0].T, expert_base, 1
    )
    extra = jnp.zeros((count * LANES,), jnp.float32)
    extra = extra.at[: docs_count * EXPERTS].set(score_part.reshape(-1))
    packed = jnp.concatenate(
        [expert_grad.reshape(count, -1, LANES), extra.reshape(count, 1, LANES)], axis=1
    )
    both = sum_all(packed, 2)
    grad_sum = both[:, :-1].reshape(docs_count, width)
    scores = both[:, -1].reshape(-1)[: docs_count * EXPERTS].reshape(docs_count, EXPERTS)
    centre = jnp.sum(doc_gates * scores, axis=1, keepdims=True)
    router_grad = doc_gates * (scores - centre)
    grad_proj = grad_sum + jnp.dot(
        router_grad, router_weight.astype(jnp.float32).T, precision=PRECISE
    )
    grad_second = jnp.dot(activated.T, grad_proj, precision=PRECISE)
    grad_hidden = lax.dot_general(
        grad_proj, w_second, (((1,), (1,)), ((), ())), precision=PRECISE
    ) * gelu_slope(pre_act)
    grad_first = jnp.dot(grad_hidden.T, embed, precision=PRECISE)
    return (mixed, grad_first, grad_second)


def solution(mesh):
    placed = (
        P(("groups", "expert"), None),
        P(),
        P("expert", None, "dp"),
        P("expert", None, "dp"),
        P("expert", "dp", None),
        P(("groups", "expert"), None),
        P("groups"),
        P("groups", None),
        P(("dp", "expert"), None),
        P(("dp", "expert"), None),
        P("groups", None),
    )
    return jax.shard_map(
        body,
        mesh=mesh,
        in_specs=placed,
        out_specs=(
            P("expert", ("groups", "dp"), None),
            P(("groups", "dp", "expert"), None),
            P(("groups", "dp", "expert"), None),
        ),
        check_vma=False,
    )
```

```python
import functools

import jax
import jax.numpy as jnp
from jax import lax
from jax.experimental import pallas as pl
from jax.experimental.pallas import tpu as pltpu
from jax.sharding import PartitionSpec as P

EXPERTS = 4
PRECISE = lax.Precision.HIGHEST
LANES = 128
FF_TILE = 512
VMEM_BYTES = 60 * 1024 * 1024


def gelu_slope(values):
    normal_cdf = 0.5 * (1.0 + jax.scipy.special.erf(values * 0.7071067811865476))
    density = jnp.exp(-0.5 * values * values) * 0.3989422804014327
    return normal_cdf + values * density


def gate_table(logits, mask):
    chosen_sum = jnp.sum(mask * logits, axis=1, keepdims=True)
    return mask * jax.nn.sigmoid(2.0 * logits - chosen_sum)


def contract_last(left, right):
    return lax.dot_general(
        left, right, (((1,), (1,)), ((), ())), preferred_element_type=jnp.float32
    )


def sum_kernel(dp_count, halves, x_ref, out_ref, land, total, sems):
    count = dp_count * halves
    me = lax.axis_index("dp") * halves + lax.axis_index("expert")

    def place(step):
        other = lax.rem(me + step, count)
        return other, {"dp": other // halves, "expert": lax.rem(other, halves)}

    barrier = pltpu.get_barrier_semaphore()
    for step in range(1, count):
        pl.semaphore_signal(
            barrier, inc=1, device_id=place(step)[1], device_id_type=pl.DeviceIdType.MESH
        )
    pl.semaphore_wait(barrier, count - 1)

    def scatter(step):
        other, device = place(step)
        return pltpu.make_async_remote_copy(
            src_ref=x_ref.at[other],
            dst_ref=land.at[step],
            send_sem=sems.at[0, step],
            recv_sem=sems.at[1, step],
            device_id=device,
            device_id_type=pl.DeviceIdType.MESH,
        )

    def spread(step):
        return pltpu.make_async_remote_copy(
            src_ref=total.at[me],
            dst_ref=total.at[me],
            send_sem=sems.at[2, step],
            recv_sem=sems.at[3, step],
            device_id=place(step)[1],
            device_id_type=pl.DeviceIdType.MESH,
        )

    for step in range(1, count):
        scatter(step).start()
    acc = x_ref[me]
    for step in range(1, count):
        scatter(step).wait_recv()
        acc = acc + land[step]
    total[me] = acc
    for step in range(1, count):
        spread(step).start()
    for step in range(1, count):
        scatter(step).wait_send()
    for step in range(1, count):
        spread(step).wait()
    out_ref[...] = total[...]


def sum_all(x, collective_id):
    dp_count = lax.axis_size("dp")
    halves = lax.axis_size("expert")
    count = dp_count * halves
    rows = x.shape[1]
    return pl.pallas_call(
        functools.partial(sum_kernel, dp_count, halves),
        out_shape=jax.ShapeDtypeStruct(x.shape, x.dtype),
        in_specs=[pl.BlockSpec(memory_space=pltpu.VMEM)],
        out_specs=pl.BlockSpec(memory_space=pltpu.VMEM),
        scratch_shapes=[
            pltpu.VMEM((count, rows, LANES), x.dtype),
            pltpu.VMEM((count, rows, LANES), x.dtype),
            pltpu.SemaphoreType.DMA((4, count)),
        ],
        compiler_params=pltpu.CompilerParams(
            collective_id=collective_id, has_side_effects=True
        ),
    )(x)


def finish_kernel(
    dp_count,
    halves,
    x_ref,
    part_ref,
    out_ref,
    mixed_ref,
    land,
    total,
    pair_land,
    near_send,
    near_land,
    far_send,
    far_land,
    sems,
    pair_sems,
    near_sems,
    far_sems,
):
    count = dp_count * halves
    groups = dp_count // 2
    dp = lax.axis_index("dp")
    half = lax.axis_index("expert")
    me = dp * halves + half
    high, low = dp // 2, lax.rem(dp, 2)

    def place(step):
        other = lax.rem(me + step, count)
        return other, {"dp": other // halves, "expert": lax.rem(other, halves)}

    barrier = pltpu.get_barrier_semaphore()
    for step in range(1, count):
        pl.semaphore_signal(
            barrier, inc=1, device_id=place(step)[1], device_id_type=pl.DeviceIdType.MESH
        )
    pl.semaphore_wait(barrier, count - 1)

    def copy(source, target, table, row, step, device):
        return pltpu.make_async_remote_copy(
            src_ref=source,
            dst_ref=target,
            send_sem=table.at[row, step],
            recv_sem=table.at[row + 1, step],
            device_id=device,
            device_id_type=pl.DeviceIdType.MESH,
        )

    def scatter(step):
        other, device = place(step)
        return copy(x_ref.at[other], land.at[step], sems, 0, step, device)

    def spread(step):
        return copy(total.at[me], total.at[me], sems, 2, step, place(step)[1])

    def goal(step, side):
        return 2 * lax.rem(high + 1 + step, groups) + side

    def pair(step, away):
        index = goal(step, (1 - low) if away else low)
        slot = step + (0 if away else groups)
        return copy(
            part_ref.at[1, index],
            pair_land.at[slot],
            pair_sems,
            0,
            slot,
            {"expert": 1 - half},
        )

    def near(step):
        return copy(
            near_send.at[step], near_land.at[step], near_sems, 0, step, {"dp": 2 * high + 1 - low}
        )

    def far(step):
        return copy(
            far_send.at[step], far_land.at[step], far_sems, 0, step, {"dp": goal(step, low)}
        )

    for step in range(1, count):
        scatter(step).start()
    for step in range(groups):
        pair(step, True).start()
    for step in range(groups):
        pair(step, False).start()
    for step in range(groups):
        pair(step, True).wait_recv()
        near_send[step] = (
            part_ref[0, goal(step, 1 - low)].astype(jnp.float32)
            + pair_land[step].astype(jnp.float32)
        ).astype(jnp.bfloat16)
        near(step).start()
    acc = x_ref[me]
    for step in range(1, count):
        scatter(step).wait_recv()
        acc = acc + land[step]
    total[me] = acc
    for step in range(1, count):
        spread(step).start()
    for step in range(groups):
        pair(step, False).wait_recv()
        near(step).wait_recv()
        block = (
            part_ref[0, goal(step, low)].astype(jnp.float32)
            + pair_land[groups + step].astype(jnp.float32)
            + near_land[step].astype(jnp.float32)
        )
        if step < groups - 1:
            far_send[step] = block.astype(jnp.bfloat16)
            far(step).start()
    for step in range(groups - 1):
        far(step).wait_recv()
        block = block + far_land[step].astype(jnp.float32)
    mixed_ref[...] = block.astype(jnp.bfloat16)
    for step in range(1, count):
        scatter(step).wait_send()
        spread(step).wait()
    out_ref[...] = total[...]
    for step in range(groups):
        pair(step, True).wait_send()
        pair(step, False).wait_send()
        near(step).wait_send()
    for step in range(groups - 1):
        far(step).wait_send()


def finish(x, part, collective_id):
    dp_count = lax.axis_size("dp")
    halves = lax.axis_size("expert")
    count = dp_count * halves
    groups = dp_count // 2
    block = part.shape[2:]
    whole = pl.BlockSpec(memory_space=pltpu.VMEM)
    return pl.pallas_call(
        functools.partial(finish_kernel, dp_count, halves),
        out_shape=(
            jax.ShapeDtypeStruct(x.shape, x.dtype),
            jax.ShapeDtypeStruct(block, jnp.bfloat16),
        ),
        in_specs=[whole, whole],
        out_specs=(whole, whole),
        scratch_shapes=[
            pltpu.VMEM(x.shape, x.dtype),
            pltpu.VMEM(x.shape, x.dtype),
            pltpu.VMEM((dp_count,) + block, jnp.bfloat16),
            pltpu.VMEM((groups,) + block, jnp.bfloat16),
            pltpu.VMEM((groups,) + block, jnp.bfloat16),
            pltpu.VMEM((groups,) + block, jnp.bfloat16),
            pltpu.VMEM((groups,) + block, jnp.bfloat16),
            pltpu.SemaphoreType.DMA((4, count)),
            pltpu.SemaphoreType.DMA((2, dp_count)),
            pltpu.SemaphoreType.DMA((2, groups)),
            pltpu.SemaphoreType.DMA((2, groups)),
        ],
        compiler_params=pltpu.CompilerParams(
            collective_id=collective_id, has_side_effects=True, vmem_limit_bytes=VMEM_BYTES
        ),
    )(x, part)


def expert_kernel(
    tok_count,
    rows_ref,
    gates_ref,
    doc_gates_ref,
    cot_ref,
    w_gate_ref,
    w_up_ref,
    w_down_ref,
    mixed_ref,
    grad_ref,
    score_ref,
    total,
):
    first = (pl.program_id(0) == 0) & (pl.program_id(1) == 0)

    @pl.when(first)
    def _():
        total[...] = jnp.zeros_like(total)
        grad_ref[...] = jnp.zeros_like(grad_ref)

    @pl.when(pl.program_id(1) == 0)
    def _():
        score_ref[...] = jnp.zeros_like(score_ref)

    rows = rows_ref[...]
    w_gate = w_gate_ref[0]
    w_up = w_up_ref[0]
    w_down = w_down_ref[0]
    gate_pre = jnp.dot(rows, w_gate, preferred_element_type=jnp.float32)
    up_pre = jnp.dot(rows, w_up, preferred_element_type=jnp.float32)
    sigma = jax.nn.sigmoid(gate_pre)
    silu = gate_pre * sigma
    product = silu * up_pre
    hidden = (product[:tok_count] * gates_ref[0]).astype(jnp.bfloat16)
    total[...] += jnp.dot(hidden, w_down, preferred_element_type=jnp.float32)
    doc_gate = gate_pre[tok_count:]
    doc_up = up_pre[tok_count:]
    doc_sigma = sigma[tok_count:]
    doc_silu = silu[tok_count:]
    doc_hidden = product[tok_count:].astype(jnp.bfloat16).astype(jnp.float32)
    back = contract_last(cot_ref[...], w_down)
    score = jnp.sum(doc_hidden * back, axis=1, keepdims=True)
    score_ref[0] += jnp.broadcast_to(score, score_ref.shape[1:])
    scaled = back * doc_gates_ref[0]
    up_grad = (scaled * doc_silu).astype(jnp.bfloat16)
    slope = doc_sigma * (1.0 + doc_gate * (1.0 - doc_sigma))
    gate_grad = (scaled * doc_up * slope).astype(jnp.bfloat16)
    grad_ref[...] += contract_last(gate_grad, w_gate) + contract_last(up_grad, w_up)

    last = (pl.program_id(0) == pl.num_programs(0) - 1) & (
        pl.program_id(1) == pl.num_programs(1) - 1
    )

    @pl.when(last)
    def _():
        mixed_ref[...] = total[...].astype(jnp.bfloat16)


def run_experts(rows, gates, doc_gates, cotangent, w_gate, w_up, w_down):
    local_count, width, ff = w_gate.shape
    tok_count = gates.shape[1]
    docs_count = cotangent.shape[0]
    tile = min(FF_TILE, ff)
    fixed = lambda e, f: (0, 0)
    of_expert = lambda e, f: (e, 0, 0)
    return pl.pallas_call(
        functools.partial(expert_kernel, tok_count),
        grid=(local_count, ff // tile),
        out_shape=(
            jax.ShapeDtypeStruct((tok_count, width), jnp.bfloat16),
            jax.ShapeDtypeStruct((docs_count, width), jnp.float32),
            jax.ShapeDtypeStruct((local_count, docs_count, LANES), jnp.float32),
        ),
        in_specs=[
            pl.BlockSpec(rows.shape, fixed),
            pl.BlockSpec((1, tok_count, 1), of_expert),
            pl.BlockSpec((1, docs_count, 1), of_expert),
            pl.BlockSpec(cotangent.shape, fixed),
            pl.BlockSpec((1, width, tile), lambda e, f: (e, 0, f)),
            pl.BlockSpec((1, width, tile), lambda e, f: (e, 0, f)),
            pl.BlockSpec((1, tile, width), lambda e, f: (e, f, 0)),
        ],
        out_specs=(
            pl.BlockSpec((tok_count, width), fixed),
            pl.BlockSpec((docs_count, width), fixed),
            pl.BlockSpec((1, docs_count, LANES), of_expert),
        ),
        scratch_shapes=[pltpu.VMEM((tok_count, width), jnp.float32)],
        compiler_params=pltpu.CompilerParams(vmem_limit_bytes=VMEM_BYTES),
    )(rows, gates, doc_gates, cotangent, w_gate, w_up, w_down)


def body(
    tokens,
    router_weight,
    w_gate,
    w_up,
    w_down,
    expert_ids,
    positions,
    embed,
    w_first,
    w_second,
    cotangent,
):
    tok_rows, width = tokens.shape
    local_count = w_gate.shape[0]
    docs_count = positions.shape[0]
    halves = lax.axis_size("expert")
    dp_count = lax.axis_size("dp")
    count = halves * dp_count
    out_rows = tok_rows // dp_count
    half = lax.axis_index("expert")
    expert_base = half * local_count
    swap = [(0, 1), (1, 0)]

    all_tokens = jnp.concatenate([tokens, lax.ppermute(tokens, "expert", swap)], axis=0)
    all_ids = jnp.concatenate([expert_ids, lax.ppermute(expert_ids, "expert", swap)], axis=0)
    span = jnp.arange(tok_rows, dtype=jnp.int32)
    row_index = jnp.concatenate([half * tok_rows + span, (1 - half) * tok_rows + span])
    expert_range = jnp.arange(EXPERTS, dtype=jnp.int32)
    choose = (all_ids[:, :, None] == expert_range[None, None, :]).astype(jnp.float32)
    route_mask = jnp.sum(choose, axis=1)
    match = (row_index[:, None] == positions[None, :]).astype(jnp.float32)
    doc_mask = jnp.dot(match.T, route_mask, precision=PRECISE)

    pre_act = lax.dot_general(embed, w_first, (((1,), (1,)), ((), ())), precision=PRECISE)
    activated = jax.nn.gelu(pre_act, approximate=False)
    partial = jnp.dot(activated, w_second, precision=PRECISE)
    projected = sum_all(partial.reshape(count, -1, LANES), 1).reshape(docs_count, width)
    doc_rows = projected.astype(jnp.bfloat16)
    placed = jnp.dot(match.astype(jnp.bfloat16), doc_rows, preferred_element_type=jnp.float32)
    present = jnp.sum(match, axis=1, keepdims=True) > 0.5
    inputs = jnp.where(present, placed.astype(jnp.bfloat16), all_tokens)
    rows = jnp.concatenate([inputs, doc_rows], axis=0)
    logits = jnp.dot(rows, router_weight, preferred_element_type=jnp.float32)
    gates = gate_table(logits, jnp.concatenate([route_mask, doc_mask], axis=0))
    own_gates = lax.dynamic_slice_in_dim(gates, expert_base, local_count, 1).T[:, :, None]
    tok_count = halves * tok_rows
    doc_gates = gates[tok_count:]

    mixed_part, expert_grad, score_local = run_experts(
        rows,
        own_gates[:, :tok_count],
        own_gates[:, tok_count:],
        cotangent,
        w_gate,
        w_up,
        w_down,
    )
    score_part = lax.dynamic_update_slice_in_dim(
        jnp.zeros((docs_count, EXPERTS), jnp.float32), score_local[:, :, 0].T, expert_base, 1
    )
    extra = jnp.zeros((count * LANES,), jnp.float32)
    extra = extra.at[: docs_count * EXPERTS].set(score_part.reshape(-1))
    packed = jnp.concatenate(
        [expert_grad.reshape(count, -1, LANES), extra.reshape(count, 1, LANES)], axis=1
    )
    both, scattered = finish(
        packed, mixed_part.reshape(halves, dp_count, out_rows, width), 2
    )
    mixed = scattered.reshape(1, out_rows, width)
    grad_sum = both[:, :-1].reshape(docs_count, width)
    scores = both[:, -1].reshape(-1)[: docs_count * EXPERTS].reshape(docs_count, EXPERTS)
    centre = jnp.sum(doc_gates * scores, axis=1, keepdims=True)
    router_grad = doc_gates * (scores - centre)
    grad_proj = grad_sum + jnp.dot(
        router_grad, router_weight.astype(jnp.float32).T, precision=PRECISE
    )
    grad_second = jnp.dot(activated.T, grad_proj, precision=PRECISE)
    grad_hidden = lax.dot_general(
        grad_proj, w_second, (((1,), (1,)), ((), ())), precision=PRECISE
    ) * gelu_slope(pre_act)
    grad_first = jnp.dot(grad_hidden.T, embed, precision=PRECISE)
    return (mixed, grad_first, grad_second)


def solution(mesh):
    placed = (
        P(("groups", "expert"), None),
        P(),
        P("expert", None, "dp"),
        P("expert", None, "dp"),
        P("expert", "dp", None),
        P(("groups", "expert"), None),
        P("groups"),
        P("groups", None),
        P(("dp", "expert"), None),
        P(("dp", "expert"), None),
        P("groups", None),
    )
    return jax.shard_map(
        body,
        mesh=mesh,
        in_specs=placed,
        out_specs=(
            P("expert", ("groups", "dp"), None),
            P(("groups", "dp", "expert"), None),
            P(("groups", "dp", "expert"), None),
        ),
        check_vma=False,
    )
```

```python
import functools

import jax
import jax.numpy as jnp
from jax import lax
from jax.experimental import pallas as pl
from jax.experimental.pallas import tpu as pltpu
from jax.sharding import PartitionSpec as P

EXPERTS = 4
PRECISE = lax.Precision.HIGHEST
LANES = 128
FF_TILE = 512
VMEM_BYTES = 60 * 1024 * 1024


def gelu_slope(values):
    normal_cdf = 0.5 * (1.0 + jax.scipy.special.erf(values * 0.7071067811865476))
    density = jnp.exp(-0.5 * values * values) * 0.3989422804014327
    return normal_cdf + values * density


def gate_table(logits, mask):
    chosen_sum = jnp.sum(mask * logits, axis=1, keepdims=True)
    return mask * jax.nn.sigmoid(2.0 * logits - chosen_sum)


def contract_last(left, right):
    return lax.dot_general(
        left, right, (((1,), (1,)), ((), ())), preferred_element_type=jnp.float32
    )


def sum_kernel(groups, x_ref, out_ref, near_land, part, far_land, total, near_sems, far_sems):
    dp = lax.axis_index("dp")
    half = lax.axis_index("expert")
    high = dp // 2
    low = lax.rem(dp, 2)
    own = low * 2 + half

    def near_place(step):
        other = lax.rem(own + step, 4)
        return other, {"dp": high * 2 + other // 2, "expert": lax.rem(other, 2)}

    def far_place(step):
        other = lax.rem(high + step, groups)
        return other, {"dp": other * 2 + low}

    barrier = pltpu.get_barrier_semaphore()
    for step in range(1, 4):
        pl.semaphore_signal(
            barrier, inc=1, device_id=near_place(step)[1], device_id_type=pl.DeviceIdType.MESH
        )
    for step in range(1, groups):
        pl.semaphore_signal(
            barrier, inc=1, device_id=far_place(step)[1], device_id_type=pl.DeviceIdType.MESH
        )
    pl.semaphore_wait(barrier, 3 + groups - 1)

    def copy(source, target, table, row, step, device):
        return pltpu.make_async_remote_copy(
            src_ref=source,
            dst_ref=target,
            send_sem=table.at[row, step],
            recv_sem=table.at[row + 1, step],
            device_id=device,
            device_id_type=pl.DeviceIdType.MESH,
        )

    def near_scatter(step):
        other, device = near_place(step)
        return copy(x_ref.at[other], near_land.at[step], near_sems, 0, step, device)

    def far_scatter(step):
        other, device = far_place(step)
        return copy(part.at[other], far_land.at[step], far_sems, 0, step, device)

    def far_spread(step):
        piece = total.at[own, high]
        return copy(piece, piece, far_sems, 2, step, far_place(step)[1])

    def near_spread(step):
        piece = total.at[own]
        return copy(piece, piece, near_sems, 2, step, near_place(step)[1])

    for step in range(1, 4):
        near_scatter(step).start()
    acc = x_ref[own]
    for step in range(1, 4):
        near_scatter(step).wait_recv()
        acc = acc + near_land[step]
    part[...] = acc
    for step in range(1, groups):
        far_scatter(step).start()
    piece = part[high]
    for step in range(1, groups):
        far_scatter(step).wait_recv()
        piece = piece + far_land[step]
    total[own, high] = piece
    for step in range(1, groups):
        far_spread(step).start()
    for step in range(1, groups):
        far_spread(step).wait_recv()
    for step in range(1, 4):
        near_spread(step).start()
    for step in range(1, 4):
        near_scatter(step).wait_send()
    for step in range(1, groups):
        far_scatter(step).wait_send()
        far_spread(step).wait_send()
    for step in range(1, 4):
        near_spread(step).wait()
    out_ref[...] = total[...]


def sum_all(x, collective_id):
    groups = lax.axis_size("dp") // 2
    x = x.reshape((4, groups) + x.shape[1:])
    return pl.pallas_call(
        functools.partial(sum_kernel, groups),
        out_shape=jax.ShapeDtypeStruct(x.shape, x.dtype),
        in_specs=[pl.BlockSpec(memory_space=pltpu.VMEM)],
        out_specs=pl.BlockSpec(memory_space=pltpu.VMEM),
        scratch_shapes=[
            pltpu.VMEM(x.shape, x.dtype),
            pltpu.VMEM(x.shape[1:], x.dtype),
            pltpu.VMEM(x.shape[1:], x.dtype),
            pltpu.VMEM(x.shape, x.dtype),
            pltpu.SemaphoreType.DMA((4, 4)),
            pltpu.SemaphoreType.DMA((4, groups)),
        ],
        compiler_params=pltpu.CompilerParams(
            collective_id=collective_id, has_side_effects=True
        ),
    )(x)


def finish_kernel(
    dp_count,
    halves,
    x_ref,
    part_ref,
    out_ref,
    mixed_ref,
    land,
    total,
    pair_land,
    near_send,
    near_land,
    far_send,
    far_land,
    sems,
    pair_sems,
    near_sems,
    far_sems,
):
    count = dp_count * halves
    groups = dp_count // 2
    dp = lax.axis_index("dp")
    half = lax.axis_index("expert")
    me = dp * halves + half
    high, low = dp // 2, lax.rem(dp, 2)

    def place(step):
        other = lax.rem(me + step, count)
        return other, {"dp": other // halves, "expert": lax.rem(other, halves)}

    barrier = pltpu.get_barrier_semaphore()
    for step in range(1, count):
        pl.semaphore_signal(
            barrier, inc=1, device_id=place(step)[1], device_id_type=pl.DeviceIdType.MESH
        )
    pl.semaphore_wait(barrier, count - 1)

    def copy(source, target, table, row, step, device):
        return pltpu.make_async_remote_copy(
            src_ref=source,
            dst_ref=target,
            send_sem=table.at[row, step],
            recv_sem=table.at[row + 1, step],
            device_id=device,
            device_id_type=pl.DeviceIdType.MESH,
        )

    def scatter(step):
        other, device = place(step)
        return copy(x_ref.at[other], land.at[step], sems, 0, step, device)

    def spread(step):
        return copy(total.at[me], total.at[me], sems, 2, step, place(step)[1])

    def goal(step, side):
        return 2 * lax.rem(high + 1 + step, groups) + side

    def pair(step, away):
        index = goal(step, (1 - low) if away else low)
        slot = step + (0 if away else groups)
        return copy(
            part_ref.at[1, index],
            pair_land.at[slot],
            pair_sems,
            0,
            slot,
            {"expert": 1 - half},
        )

    def near(step):
        return copy(
            near_send.at[step], near_land.at[step], near_sems, 0, step, {"dp": 2 * high + 1 - low}
        )

    def far(step):
        return copy(
            far_send.at[step], far_land.at[step], far_sems, 0, step, {"dp": goal(step, low)}
        )

    for step in range(1, count):
        scatter(step).start()
    for step in range(groups):
        pair(step, True).start()
    for step in range(groups):
        pair(step, False).start()
    for step in range(groups):
        pair(step, True).wait_recv()
        near_send[step] = (
            part_ref[0, goal(step, 1 - low)].astype(jnp.float32)
            + pair_land[step].astype(jnp.float32)
        ).astype(jnp.bfloat16)
        near(step).start()
    acc = x_ref[me]
    for step in range(1, count):
        scatter(step).wait_recv()
        acc = acc + land[step]
    total[me] = acc
    for step in range(1, count):
        spread(step).start()
    for step in range(groups):
        pair(step, False).wait_recv()
        near(step).wait_recv()
        block = (
            part_ref[0, goal(step, low)].astype(jnp.float32)
            + pair_land[groups + step].astype(jnp.float32)
            + near_land[step].astype(jnp.float32)
        )
        if step < groups - 1:
            far_send[step] = block.astype(jnp.bfloat16)
            far(step).start()
    for step in range(groups - 1):
        far(step).wait_recv()
        block = block + far_land[step].astype(jnp.float32)
    mixed_ref[...] = block.astype(jnp.bfloat16)
    for step in range(1, count):
        scatter(step).wait_send()
        spread(step).wait()
    out_ref[...] = total[...]
    for step in range(groups):
        pair(step, True).wait_send()
        pair(step, False).wait_send()
        near(step).wait_send()
    for step in range(groups - 1):
        far(step).wait_send()


def finish(x, part, collective_id):
    dp_count = lax.axis_size("dp")
    halves = lax.axis_size("expert")
    count = dp_count * halves
    groups = dp_count // 2
    block = part.shape[2:]
    whole = pl.BlockSpec(memory_space=pltpu.VMEM)
    return pl.pallas_call(
        functools.partial(finish_kernel, dp_count, halves),
        out_shape=(
            jax.ShapeDtypeStruct(x.shape, x.dtype),
            jax.ShapeDtypeStruct(block, jnp.bfloat16),
        ),
        in_specs=[whole, whole],
        out_specs=(whole, whole),
        scratch_shapes=[
            pltpu.VMEM(x.shape, x.dtype),
            pltpu.VMEM(x.shape, x.dtype),
            pltpu.VMEM((dp_count,) + block, jnp.bfloat16),
            pltpu.VMEM((groups,) + block, jnp.bfloat16),
            pltpu.VMEM((groups,) + block, jnp.bfloat16),
            pltpu.VMEM((groups,) + block, jnp.bfloat16),
            pltpu.VMEM((groups,) + block, jnp.bfloat16),
            pltpu.SemaphoreType.DMA((4, count)),
            pltpu.SemaphoreType.DMA((2, dp_count)),
            pltpu.SemaphoreType.DMA((2, groups)),
            pltpu.SemaphoreType.DMA((2, groups)),
        ],
        compiler_params=pltpu.CompilerParams(
            collective_id=collective_id, has_side_effects=True, vmem_limit_bytes=VMEM_BYTES
        ),
    )(x, part)


def expert_kernel(
    tok_count,
    rows_ref,
    gates_ref,
    doc_gates_ref,
    cot_ref,
    w_gate_ref,
    w_up_ref,
    w_down_ref,
    mixed_ref,
    grad_ref,
    score_ref,
    total,
):
    first = (pl.program_id(0) == 0) & (pl.program_id(1) == 0)

    @pl.when(first)
    def _():
        total[...] = jnp.zeros_like(total)
        grad_ref[...] = jnp.zeros_like(grad_ref)

    @pl.when(pl.program_id(1) == 0)
    def _():
        score_ref[...] = jnp.zeros_like(score_ref)

    rows = rows_ref[...]
    w_gate = w_gate_ref[0]
    w_up = w_up_ref[0]
    w_down = w_down_ref[0]
    gate_pre = jnp.dot(rows, w_gate, preferred_element_type=jnp.float32)
    up_pre = jnp.dot(rows, w_up, preferred_element_type=jnp.float32)
    sigma = jax.nn.sigmoid(gate_pre)
    silu = gate_pre * sigma
    product = silu * up_pre
    hidden = (product[:tok_count] * gates_ref[0]).astype(jnp.bfloat16)
    total[...] += jnp.dot(hidden, w_down, preferred_element_type=jnp.float32)
    doc_gate = gate_pre[tok_count:]
    doc_up = up_pre[tok_count:]
    doc_sigma = sigma[tok_count:]
    doc_silu = silu[tok_count:]
    doc_hidden = product[tok_count:].astype(jnp.bfloat16).astype(jnp.float32)
    back = contract_last(cot_ref[...], w_down)
    score = jnp.sum(doc_hidden * back, axis=1, keepdims=True)
    score_ref[0] += jnp.broadcast_to(score, score_ref.shape[1:])
    scaled = back * doc_gates_ref[0]
    up_grad = (scaled * doc_silu).astype(jnp.bfloat16)
    slope = doc_sigma * (1.0 + doc_gate * (1.0 - doc_sigma))
    gate_grad = (scaled * doc_up * slope).astype(jnp.bfloat16)
    grad_ref[...] += contract_last(gate_grad, w_gate) + contract_last(up_grad, w_up)

    last = (pl.program_id(0) == pl.num_programs(0) - 1) & (
        pl.program_id(1) == pl.num_programs(1) - 1
    )

    @pl.when(last)
    def _():
        mixed_ref[...] = total[...].astype(jnp.bfloat16)


def run_experts(rows, gates, doc_gates, cotangent, w_gate, w_up, w_down):
    local_count, width, ff = w_gate.shape
    tok_count = gates.shape[1]
    docs_count = cotangent.shape[0]
    tile = min(FF_TILE, ff)
    fixed = lambda e, f: (0, 0)
    of_expert = lambda e, f: (e, 0, 0)
    return pl.pallas_call(
        functools.partial(expert_kernel, tok_count),
        grid=(local_count, ff // tile),
        out_shape=(
            jax.ShapeDtypeStruct((tok_count, width), jnp.bfloat16),
            jax.ShapeDtypeStruct((docs_count, width), jnp.float32),
            jax.ShapeDtypeStruct((local_count, docs_count, LANES), jnp.float32),
        ),
        in_specs=[
            pl.BlockSpec(rows.shape, fixed),
            pl.BlockSpec((1, tok_count, 1), of_expert),
            pl.BlockSpec((1, docs_count, 1), of_expert),
            pl.BlockSpec(cotangent.shape, fixed),
            pl.BlockSpec((1, width, tile), lambda e, f: (e, 0, f)),
            pl.BlockSpec((1, width, tile), lambda e, f: (e, 0, f)),
            pl.BlockSpec((1, tile, width), lambda e, f: (e, f, 0)),
        ],
        out_specs=(
            pl.BlockSpec((tok_count, width), fixed),
            pl.BlockSpec((docs_count, width), fixed),
            pl.BlockSpec((1, docs_count, LANES), of_expert),
        ),
        scratch_shapes=[pltpu.VMEM((tok_count, width), jnp.float32)],
        compiler_params=pltpu.CompilerParams(vmem_limit_bytes=VMEM_BYTES),
    )(rows, gates, doc_gates, cotangent, w_gate, w_up, w_down)


def body(
    tokens,
    router_weight,
    w_gate,
    w_up,
    w_down,
    expert_ids,
    positions,
    embed,
    w_first,
    w_second,
    cotangent,
):
    tok_rows, width = tokens.shape
    local_count = w_gate.shape[0]
    docs_count = positions.shape[0]
    halves = lax.axis_size("expert")
    dp_count = lax.axis_size("dp")
    count = halves * dp_count
    out_rows = tok_rows // dp_count
    half = lax.axis_index("expert")
    expert_base = half * local_count
    swap = [(0, 1), (1, 0)]

    all_tokens = jnp.concatenate([tokens, lax.ppermute(tokens, "expert", swap)], axis=0)
    all_ids = jnp.concatenate([expert_ids, lax.ppermute(expert_ids, "expert", swap)], axis=0)
    span = jnp.arange(tok_rows, dtype=jnp.int32)
    row_index = jnp.concatenate([half * tok_rows + span, (1 - half) * tok_rows + span])
    expert_range = jnp.arange(EXPERTS, dtype=jnp.int32)
    choose = (all_ids[:, :, None] == expert_range[None, None, :]).astype(jnp.float32)
    route_mask = jnp.sum(choose, axis=1)
    match = (row_index[:, None] == positions[None, :]).astype(jnp.float32)
    doc_mask = jnp.dot(match.T, route_mask, precision=PRECISE)

    pre_act = lax.dot_general(embed, w_first, (((1,), (1,)), ((), ())), precision=PRECISE)
    activated = jax.nn.gelu(pre_act, approximate=False)
    partial = jnp.dot(activated, w_second, precision=PRECISE)
    projected = sum_all(partial.reshape(count, -1, LANES), 1).reshape(docs_count, width)
    doc_rows = projected.astype(jnp.bfloat16)
    placed = jnp.dot(match.astype(jnp.bfloat16), doc_rows, preferred_element_type=jnp.float32)
    present = jnp.sum(match, axis=1, keepdims=True) > 0.5
    inputs = jnp.where(present, placed.astype(jnp.bfloat16), all_tokens)
    rows = jnp.concatenate([inputs, doc_rows], axis=0)
    logits = jnp.dot(rows, router_weight, preferred_element_type=jnp.float32)
    gates = gate_table(logits, jnp.concatenate([route_mask, doc_mask], axis=0))
    own_gates = lax.dynamic_slice_in_dim(gates, expert_base, local_count, 1).T[:, :, None]
    tok_count = halves * tok_rows
    doc_gates = gates[tok_count:]

    mixed_part, expert_grad, score_local = run_experts(
        rows,
        own_gates[:, :tok_count],
        own_gates[:, tok_count:],
        cotangent,
        w_gate,
        w_up,
        w_down,
    )
    score_part = lax.dynamic_update_slice_in_dim(
        jnp.zeros((docs_count, EXPERTS), jnp.float32), score_local[:, :, 0].T, expert_base, 1
    )
    extra = jnp.zeros((count * LANES,), jnp.float32)
    extra = extra.at[: docs_count * EXPERTS].set(score_part.reshape(-1))
    packed = jnp.concatenate(
        [expert_grad.reshape(count, -1, LANES), extra.reshape(count, 1, LANES)], axis=1
    )
    both, scattered = finish(
        packed, mixed_part.reshape(halves, dp_count, out_rows, width), 2
    )
    mixed = scattered.reshape(1, out_rows, width)
    grad_sum = both[:, :-1].reshape(docs_count, width)
    scores = both[:, -1].reshape(-1)[: docs_count * EXPERTS].reshape(docs_count, EXPERTS)
    centre = jnp.sum(doc_gates * scores, axis=1, keepdims=True)
    router_grad = doc_gates * (scores - centre)
    grad_proj = grad_sum + jnp.dot(
        router_grad, router_weight.astype(jnp.float32).T, precision=PRECISE
    )
    grad_second = jnp.dot(activated.T, grad_proj, precision=PRECISE)
    grad_hidden = lax.dot_general(
        grad_proj, w_second, (((1,), (1,)), ((), ())), precision=PRECISE
    ) * gelu_slope(pre_act)
    grad_first = jnp.dot(grad_hidden.T, embed, precision=PRECISE)
    return (mixed, grad_first, grad_second)


def solution(mesh):
    placed = (
        P(("groups", "expert"), None),
        P(),
        P("expert", None, "dp"),
        P("expert", None, "dp"),
        P("expert", "dp", None),
        P(("groups", "expert"), None),
        P("groups"),
        P("groups", None),
        P(("dp", "expert"), None),
        P(("dp", "expert"), None),
        P("groups", None),
    )
    return jax.shard_map(
        body,
        mesh=mesh,
        in_specs=placed,
        out_specs=(
            P("expert", ("groups", "dp"), None),
            P(("groups", "dp", "expert"), None),
            P(("groups", "dp", "expert"), None),
        ),
        check_vma=False,
    )
```

```python
import functools

import jax
import jax.numpy as jnp
from jax import lax
from jax.experimental import pallas as pl
from jax.experimental.pallas import tpu as pltpu
from jax.sharding import PartitionSpec as P

EXPERTS = 4
PRECISE = lax.Precision.HIGHEST
LANES = 128
FF_TILE = 512
VMEM_BYTES = 60 * 1024 * 1024


def gelu_slope(values):
    normal_cdf = 0.5 * (1.0 + jax.scipy.special.erf(values * 0.7071067811865476))
    density = jnp.exp(-0.5 * values * values) * 0.3989422804014327
    return normal_cdf + values * density


def gate_table(logits, mask):
    chosen_sum = jnp.sum(mask * logits, axis=1, keepdims=True)
    return mask * jax.nn.sigmoid(2.0 * logits - chosen_sum)


def contract_last(left, right):
    return lax.dot_general(
        left, right, (((1,), (1,)), ((), ())), preferred_element_type=jnp.float32
    )


def sum_kernel(groups, x_ref, out_ref, near_land, part, far_land, total, near_sems, far_sems):
    dp = lax.axis_index("dp")
    half = lax.axis_index("expert")
    high = dp // 2
    low = lax.rem(dp, 2)
    own = low * 2 + half

    def near_place(step):
        other = lax.rem(own + step, 4)
        return other, {"dp": high * 2 + other // 2, "expert": lax.rem(other, 2)}

    def far_place(step):
        other = lax.rem(high + step, groups)
        return other, {"dp": other * 2 + low}

    barrier = pltpu.get_barrier_semaphore()
    for step in range(1, 4):
        pl.semaphore_signal(
            barrier, inc=1, device_id=near_place(step)[1], device_id_type=pl.DeviceIdType.MESH
        )
    for step in range(1, groups):
        pl.semaphore_signal(
            barrier, inc=1, device_id=far_place(step)[1], device_id_type=pl.DeviceIdType.MESH
        )
    pl.semaphore_wait(barrier, 3 + groups - 1)

    def copy(source, target, table, row, step, device):
        return pltpu.make_async_remote_copy(
            src_ref=source,
            dst_ref=target,
            send_sem=table.at[row, step],
            recv_sem=table.at[row + 1, step],
            device_id=device,
            device_id_type=pl.DeviceIdType.MESH,
        )

    def near_scatter(step):
        other, device = near_place(step)
        return copy(x_ref.at[other], near_land.at[step], near_sems, 0, step, device)

    def far_scatter(step):
        other, device = far_place(step)
        return copy(part.at[other], far_land.at[step], far_sems, 0, step, device)

    def far_spread(step):
        piece = total.at[own, high]
        return copy(piece, piece, far_sems, 2, step, far_place(step)[1])

    def near_spread(step):
        piece = total.at[own]
        return copy(piece, piece, near_sems, 2, step, near_place(step)[1])

    for step in range(1, 4):
        near_scatter(step).start()
    acc = x_ref[own]
    for step in range(1, 4):
        near_scatter(step).wait_recv()
        acc = acc + near_land[step]
    part[...] = acc
    for step in range(1, groups):
        far_scatter(step).start()
    piece = part[high]
    for step in range(1, groups):
        far_scatter(step).wait_recv()
        piece = piece + far_land[step]
    total[own, high] = piece
    for step in range(1, groups):
        far_spread(step).start()
    for step in range(1, groups):
        far_spread(step).wait_recv()
    for step in range(1, 4):
        near_spread(step).start()
    for step in range(1, 4):
        near_scatter(step).wait_send()
    for step in range(1, groups):
        far_scatter(step).wait_send()
        far_spread(step).wait_send()
    for step in range(1, 4):
        near_spread(step).wait()
    out_ref[...] = total[...]


def sum_all(x, collective_id):
    groups = lax.axis_size("dp") // 2
    x = x.reshape((4, groups) + x.shape[1:])
    return pl.pallas_call(
        functools.partial(sum_kernel, groups),
        out_shape=jax.ShapeDtypeStruct(x.shape, x.dtype),
        in_specs=[pl.BlockSpec(memory_space=pltpu.VMEM)],
        out_specs=pl.BlockSpec(memory_space=pltpu.VMEM),
        scratch_shapes=[
            pltpu.VMEM(x.shape, x.dtype),
            pltpu.VMEM(x.shape[1:], x.dtype),
            pltpu.VMEM(x.shape[1:], x.dtype),
            pltpu.VMEM(x.shape, x.dtype),
            pltpu.SemaphoreType.DMA((4, 4)),
            pltpu.SemaphoreType.DMA((4, groups)),
        ],
        compiler_params=pltpu.CompilerParams(
            collective_id=collective_id, has_side_effects=True
        ),
    )(x)


def finish_kernel(
    dp_count,
    halves,
    x_ref,
    part_ref,
    out_ref,
    mixed_ref,
    land,
    total,
    pair_land,
    near_send,
    near_land,
    far_send,
    far_land,
    sems,
    pair_sems,
    near_sems,
    far_sems,
):
    count = dp_count * halves
    groups = dp_count // 2
    dp = lax.axis_index("dp")
    half = lax.axis_index("expert")
    me = dp * halves + half
    high, low = dp // 2, lax.rem(dp, 2)

    def place(step):
        other = lax.rem(me + step, count)
        return other, {"dp": other // halves, "expert": lax.rem(other, halves)}

    barrier = pltpu.get_barrier_semaphore()
    for step in range(1, count):
        pl.semaphore_signal(
            barrier, inc=1, device_id=place(step)[1], device_id_type=pl.DeviceIdType.MESH
        )
    pl.semaphore_wait(barrier, count - 1)

    def copy(source, target, table, row, step, device):
        return pltpu.make_async_remote_copy(
            src_ref=source,
            dst_ref=target,
            send_sem=table.at[row, step],
            recv_sem=table.at[row + 1, step],
            device_id=device,
            device_id_type=pl.DeviceIdType.MESH,
        )

    def scatter(step):
        other, device = place(step)
        return copy(x_ref.at[other], land.at[step], sems, 0, step, device)

    def spread(step):
        return copy(total.at[me], total.at[me], sems, 2, step, place(step)[1])

    def goal(step, side):
        return 2 * lax.rem(high + 1 + step, groups) + side

    def pair(step, away):
        index = goal(step, (1 - low) if away else low)
        slot = step + (0 if away else groups)
        return copy(
            part_ref.at[1, index],
            pair_land.at[slot],
            pair_sems,
            0,
            slot,
            {"expert": 1 - half},
        )

    def near(step):
        return copy(
            near_send.at[step], near_land.at[step], near_sems, 0, step, {"dp": 2 * high + 1 - low}
        )

    def far(step):
        return copy(
            far_send.at[step], far_land.at[step], far_sems, 0, step, {"dp": goal(step, low)}
        )

    for step in range(groups):
        pair(step, True).start()
    for step in range(1, count):
        scatter(step).start()
    for step in range(groups):
        pair(step, False).start()
    for step in range(groups):
        pair(step, True).wait_recv()
        near_send[step] = (
            part_ref[0, goal(step, 1 - low)].astype(jnp.float32)
            + pair_land[step].astype(jnp.float32)
        ).astype(jnp.bfloat16)
        near(step).start()
    acc = x_ref[me]
    for step in range(1, count):
        scatter(step).wait_recv()
        acc = acc + land[step]
    total[me] = acc
    for step in range(1, count):
        spread(step).start()
    for step in range(groups):
        pair(step, False).wait_recv()
        near(step).wait_recv()
        block = (
            part_ref[0, goal(step, low)].astype(jnp.float32)
            + pair_land[groups + step].astype(jnp.float32)
            + near_land[step].astype(jnp.float32)
        )
        if step < groups - 1:
            far_send[step] = block.astype(jnp.bfloat16)
            far(step).start()
    for step in range(groups - 1):
        far(step).wait_recv()
        block = block + far_land[step].astype(jnp.float32)
    mixed_ref[...] = block.astype(jnp.bfloat16)
    for step in range(1, count):
        scatter(step).wait_send()
        spread(step).wait()
    out_ref[...] = total[...]
    for step in range(groups):
        pair(step, True).wait_send()
        pair(step, False).wait_send()
        near(step).wait_send()
    for step in range(groups - 1):
        far(step).wait_send()


def finish(x, part, collective_id):
    dp_count = lax.axis_size("dp")
    halves = lax.axis_size("expert")
    count = dp_count * halves
    groups = dp_count // 2
    block = part.shape[2:]
    whole = pl.BlockSpec(memory_space=pltpu.VMEM)
    return pl.pallas_call(
        functools.partial(finish_kernel, dp_count, halves),
        out_shape=(
            jax.ShapeDtypeStruct(x.shape, x.dtype),
            jax.ShapeDtypeStruct(block, jnp.bfloat16),
        ),
        in_specs=[whole, whole],
        out_specs=(whole, whole),
        scratch_shapes=[
            pltpu.VMEM(x.shape, x.dtype),
            pltpu.VMEM(x.shape, x.dtype),
            pltpu.VMEM((dp_count,) + block, jnp.bfloat16),
            pltpu.VMEM((groups,) + block, jnp.bfloat16),
            pltpu.VMEM((groups,) + block, jnp.bfloat16),
            pltpu.VMEM((groups,) + block, jnp.bfloat16),
            pltpu.VMEM((groups,) + block, jnp.bfloat16),
            pltpu.SemaphoreType.DMA((4, count)),
            pltpu.SemaphoreType.DMA((2, dp_count)),
            pltpu.SemaphoreType.DMA((2, groups)),
            pltpu.SemaphoreType.DMA((2, groups)),
        ],
        compiler_params=pltpu.CompilerParams(
            collective_id=collective_id, has_side_effects=True, vmem_limit_bytes=VMEM_BYTES
        ),
    )(x, part)


def expert_kernel(
    tok_count,
    rows_ref,
    gates_ref,
    doc_gates_ref,
    cot_ref,
    w_gate_ref,
    w_up_ref,
    w_down_ref,
    mixed_ref,
    grad_ref,
    score_ref,
    total,
):
    first = (pl.program_id(0) == 0) & (pl.program_id(1) == 0)

    @pl.when(first)
    def _():
        total[...] = jnp.zeros_like(total)
        grad_ref[...] = jnp.zeros_like(grad_ref)

    @pl.when(pl.program_id(1) == 0)
    def _():
        score_ref[...] = jnp.zeros_like(score_ref)

    rows = rows_ref[...]
    w_gate = w_gate_ref[0]
    w_up = w_up_ref[0]
    w_down = w_down_ref[0]
    gate_pre = jnp.dot(rows, w_gate, preferred_element_type=jnp.float32)
    up_pre = jnp.dot(rows, w_up, preferred_element_type=jnp.float32)
    sigma = jax.nn.sigmoid(gate_pre)
    silu = gate_pre * sigma
    product = silu * up_pre
    hidden = (product[:tok_count] * gates_ref[0]).astype(jnp.bfloat16)
    total[...] += jnp.dot(hidden, w_down, preferred_element_type=jnp.float32)
    doc_gate = gate_pre[tok_count:]
    doc_up = up_pre[tok_count:]
    doc_sigma = sigma[tok_count:]
    doc_silu = silu[tok_count:]
    doc_hidden = product[tok_count:].astype(jnp.bfloat16).astype(jnp.float32)
    back = contract_last(cot_ref[...], w_down)
    score = jnp.sum(doc_hidden * back, axis=1, keepdims=True)
    score_ref[0] += jnp.broadcast_to(score, score_ref.shape[1:])
    scaled = back * doc_gates_ref[0]
    up_grad = (scaled * doc_silu).astype(jnp.bfloat16)
    slope = doc_sigma * (1.0 + doc_gate * (1.0 - doc_sigma))
    gate_grad = (scaled * doc_up * slope).astype(jnp.bfloat16)
    grad_ref[...] += contract_last(gate_grad, w_gate) + contract_last(up_grad, w_up)

    last = (pl.program_id(0) == pl.num_programs(0) - 1) & (
        pl.program_id(1) == pl.num_programs(1) - 1
    )

    @pl.when(last)
    def _():
        mixed_ref[...] = total[...].astype(jnp.bfloat16)


def run_experts(rows, gates, doc_gates, cotangent, w_gate, w_up, w_down):
    local_count, width, ff = w_gate.shape
    tok_count = gates.shape[1]
    docs_count = cotangent.shape[0]
    tile = min(FF_TILE, ff)
    fixed = lambda e, f: (0, 0)
    of_expert = lambda e, f: (e, 0, 0)
    return pl.pallas_call(
        functools.partial(expert_kernel, tok_count),
        grid=(local_count, ff // tile),
        out_shape=(
            jax.ShapeDtypeStruct((tok_count, width), jnp.bfloat16),
            jax.ShapeDtypeStruct((docs_count, width), jnp.float32),
            jax.ShapeDtypeStruct((local_count, docs_count, LANES), jnp.float32),
        ),
        in_specs=[
            pl.BlockSpec(rows.shape, fixed),
            pl.BlockSpec((1, tok_count, 1), of_expert),
            pl.BlockSpec((1, docs_count, 1), of_expert),
            pl.BlockSpec(cotangent.shape, fixed),
            pl.BlockSpec((1, width, tile), lambda e, f: (e, 0, f)),
            pl.BlockSpec((1, width, tile), lambda e, f: (e, 0, f)),
            pl.BlockSpec((1, tile, width), lambda e, f: (e, f, 0)),
        ],
        out_specs=(
            pl.BlockSpec((tok_count, width), fixed),
            pl.BlockSpec((docs_count, width), fixed),
            pl.BlockSpec((1, docs_count, LANES), of_expert),
        ),
        scratch_shapes=[pltpu.VMEM((tok_count, width), jnp.float32)],
        compiler_params=pltpu.CompilerParams(vmem_limit_bytes=VMEM_BYTES),
    )(rows, gates, doc_gates, cotangent, w_gate, w_up, w_down)


def body(
    tokens,
    router_weight,
    w_gate,
    w_up,
    w_down,
    expert_ids,
    positions,
    embed,
    w_first,
    w_second,
    cotangent,
):
    tok_rows, width = tokens.shape
    local_count = w_gate.shape[0]
    docs_count = positions.shape[0]
    halves = lax.axis_size("expert")
    dp_count = lax.axis_size("dp")
    count = halves * dp_count
    out_rows = tok_rows // dp_count
    half = lax.axis_index("expert")
    expert_base = half * local_count
    swap = [(0, 1), (1, 0)]

    all_tokens = jnp.concatenate([tokens, lax.ppermute(tokens, "expert", swap)], axis=0)
    all_ids = jnp.concatenate([expert_ids, lax.ppermute(expert_ids, "expert", swap)], axis=0)
    span = jnp.arange(tok_rows, dtype=jnp.int32)
    row_index = jnp.concatenate([half * tok_rows + span, (1 - half) * tok_rows + span])
    expert_range = jnp.arange(EXPERTS, dtype=jnp.int32)
    choose = (all_ids[:, :, None] == expert_range[None, None, :]).astype(jnp.float32)
    route_mask = jnp.sum(choose, axis=1)
    match = (row_index[:, None] == positions[None, :]).astype(jnp.float32)
    doc_mask = jnp.dot(match.T, route_mask, precision=PRECISE)

    pre_act = lax.dot_general(embed, w_first, (((1,), (1,)), ((), ())), precision=PRECISE)
    activated = jax.nn.gelu(pre_act, approximate=False)
    partial = jnp.dot(activated, w_second, precision=PRECISE)
    projected = sum_all(partial.reshape(count, -1, LANES), 1).reshape(docs_count, width)
    doc_rows = projected.astype(jnp.bfloat16)
    placed = jnp.dot(match.astype(jnp.bfloat16), doc_rows, preferred_element_type=jnp.float32)
    present = jnp.sum(match, axis=1, keepdims=True) > 0.5
    inputs = jnp.where(present, placed.astype(jnp.bfloat16), all_tokens)
    rows = jnp.concatenate([inputs, doc_rows], axis=0)
    logits = jnp.dot(rows, router_weight, preferred_element_type=jnp.float32)
    gates = gate_table(logits, jnp.concatenate([route_mask, doc_mask], axis=0))
    own_gates = lax.dynamic_slice_in_dim(gates, expert_base, local_count, 1).T[:, :, None]
    tok_count = halves * tok_rows
    doc_gates = gates[tok_count:]

    mixed_part, expert_grad, score_local = run_experts(
        rows,
        own_gates[:, :tok_count],
        own_gates[:, tok_count:],
        cotangent,
        w_gate,
        w_up,
        w_down,
    )
    score_part = lax.dynamic_update_slice_in_dim(
        jnp.zeros((docs_count, EXPERTS), jnp.float32), score_local[:, :, 0].T, expert_base, 1
    )
    extra = jnp.zeros((count * LANES,), jnp.float32)
    extra = extra.at[: docs_count * EXPERTS].set(score_part.reshape(-1))
    packed = jnp.concatenate(
        [expert_grad.reshape(count, -1, LANES), extra.reshape(count, 1, LANES)], axis=1
    )
    both, scattered = finish(
        packed, mixed_part.reshape(halves, dp_count, out_rows, width), 2
    )
    mixed = scattered.reshape(1, out_rows, width)
    grad_sum = both[:, :-1].reshape(docs_count, width)
    scores = both[:, -1].reshape(-1)[: docs_count * EXPERTS].reshape(docs_count, EXPERTS)
    centre = jnp.sum(doc_gates * scores, axis=1, keepdims=True)
    router_grad = doc_gates * (scores - centre)
    grad_proj = grad_sum + jnp.dot(
        router_grad, router_weight.astype(jnp.float32).T, precision=PRECISE
    )
    grad_second = jnp.dot(activated.T, grad_proj, precision=PRECISE)
    grad_hidden = lax.dot_general(
        grad_proj, w_second, (((1,), (1,)), ((), ())), precision=PRECISE
    ) * gelu_slope(pre_act)
    grad_first = jnp.dot(grad_hidden.T, embed, precision=PRECISE)
    return (mixed, grad_first, grad_second)


def solution(mesh):
    placed = (
        P(("groups", "expert"), None),
        P(),
        P("expert", None, "dp"),
        P("expert", None, "dp"),
        P("expert", "dp", None),
        P(("groups", "expert"), None),
        P("groups"),
        P("groups", None),
        P(("dp", "expert"), None),
        P(("dp", "expert"), None),
        P("groups", None),
    )
    return jax.shard_map(
        body,
        mesh=mesh,
        in_specs=placed,
        out_specs=(
            P("expert", ("groups", "dp"), None),
            P(("groups", "dp", "expert"), None),
            P(("groups", "dp", "expert"), None),
        ),
        check_vma=False,
    )
```
